128 devices in a mesh: dp: 2 (over core), segment: 2 (over x_hi), tensor: 32 (over y, x_lo, z).
Axes of the slice: x: 4 (x_hi: 2, x_lo: 2; x = x_hi * 2 + x_lo), y: 4, z: 4, core: 2. Of those that a mesh axis runs over, the one named last changes fastest.
Arguments:
- hidden_state: bfloat16 [256, 16384], P('dp', 'tensor'), parts along dimension 0, may hold values from -6 to 6
- norm_gain: bfloat16 [2, 16384], P('segment'), may hold values from 0.099609375 to 1.8984375
- w_query: bfloat16 [2, 16384, 8192], P('segment', None, 'tensor'), may hold values from -0.046875 to 0.046875
- w_key_value: bfloat16 [2, 16384, 1024], P('segment', 'tensor'), may hold values from -0.046875 to 0.046875
- w_output: bfloat16 [2, 8192, 16384], P('segment', 'tensor'), may hold values from -0.5 to 0.5
- kv_cache: bfloat16 [2, 256, 2, 4, 2048, 128], P('segment', ('dp', 'tensor')), parts along dimension 1, may hold values from -250 to 250
- context_len: int32 [256], P('dp'), parts along dimension 0, may hold values from 2 to 2048, as said below
Outputs:
- section_out: bfloat16 [2, 256, 16384], P('segment', 'dp', 'tensor'), parts along dimension 1
The draws below stay inside these ranges and needn't reach their ends.
There are 2 independent parts, one for each index of `dp`. The reference program is written for one: setup_inputs(seed, part) draws one part's arguments, and reference() takes and returns one part's arrays. A program takes and returns all parts, laid end to end along the dimension named above; an argument that names none is the same for every part. Nothing has to cross between parts.
Inputs may be any that keep to these rules, and one draw needn't show every extreme that they name: `context_len`: each row's context length; at least one row has the full 4 * 512.
All inputs are finite; a program needn't handle non-finite values.
Results may differ from the reference program's by a relative error of at most 0.015.
The reference program's roundings to bfloat16 on the way count: a program that leaves them out, or rounds other values in their place, can miss the bound.
Values may be sent and summed in bfloat16 or wider, within the bound.
A program may use at most 192 MiB of HBM per device.

```python
import jax
import jax.numpy as jnp
from jax import lax

D = 16384
HEADS = 64
KVH = 4
HD = 128
TILE = 512
TILES = 4
ROWS = 128


def draw_context_len(key, part):
    key = jax.random.fold_in(key, 1)
    first_key, second_key, third_key = jax.random.split(key, 3)
    longest = TILES * TILE
    first = jax.random.randint(first_key, (ROWS,), 2, longest + 1, dtype=jnp.int32)
    second = jax.random.randint(second_key, (ROWS,), 2, longest + 1, dtype=jnp.int32)
    lengths = jnp.minimum(first, second)
    chosen = jax.random.randint(third_key, (), 0, ROWS, dtype=jnp.int32)
    return lengths.at[chosen].set(longest)


def draw_kv_cache(key, part):
    key = jax.random.fold_in(key, 2)
    shape = (2, ROWS, 2, KVH, TILES * TILE, HD)
    return jax.random.truncated_normal(key, -4.0, 4.0, shape).astype(jnp.bfloat16)


def block_levels(key, dims, cuts, smallest, largest):
    def one(dim, blocks):
        draws = jax.random.uniform(jax.random.fold_in(jax.random.fold_in(key, 6), dim), (blocks,), jnp.float32, smallest / len(cuts), largest / len(cuts))
        return jnp.repeat(jnp.exp(draws), dims[dim] // blocks).reshape((-1,) + (1,) * (len(dims) - dim - 1))

    level = one(*cuts[0])
    for cut in cuts[1:]:
        level = level * one(*cut)
    return level


def gaussian(rng, extent, width, reach, cuts=(), held_as=jnp.bfloat16):
    entries = width * jax.random.normal(rng, extent, jnp.float32)
    if cuts:
        entries = entries * block_levels(rng, extent, cuts, -0.22, 0.18)
    return jnp.clip(entries, -reach, reach).astype(held_as)


def setup_inputs(seed: int = 0, part: int = 0) -> dict:
    arg_keys = jax.random.split(jax.random.key(seed), 8)
    own_keys = jax.random.split(jax.random.fold_in(arg_keys[7], part), 8)
    return {
        "hidden_state": gaussian(own_keys[0], (ROWS, D), 1.0, 6.0, ((1, 32),)),
        "norm_gain": jnp.clip(1.0 + 0.18 * jax.random.normal(arg_keys[1], (2, D), jnp.float32), 0.099609375, 1.8984375).astype(jnp.bfloat16),
        "w_query": gaussian(arg_keys[2], (2, D, HEADS * HD), D ** -0.5, 0.046875, ((0, 2), (2, 32))),
        "w_key_value": gaussian(arg_keys[3], (2, D, 2 * KVH * HD), D ** -0.5, 0.046875, ((0, 2), (1, 32))),
        "w_output": gaussian(arg_keys[4], (2, HEADS * HD, D), HD ** -0.5, 0.5, ((0, 2), (1, 32))),
        "kv_cache": draw_kv_cache(jax.random.fold_in(jax.random.fold_in(arg_keys[7], part), 71), part),
        "context_len": draw_context_len(jax.random.fold_in(jax.random.fold_in(arg_keys[7], part), 71), part),
    }


epsilon = 1e-05
masked_value = -1e+30

def normalize(inputs, gain):
    values = inputs.astype(jnp.float32)
    mean_square = lax.optimization_barrier(jnp.mean(values * values, axis=-1, keepdims=True))
    return (values * jax.lax.rsqrt(mean_square + epsilon) * gain.astype(jnp.float32)).astype(jnp.bfloat16)

def attend(queries, new_entries, keys, values, context_len):
    rows = queries.shape[0]
    grouped = queries.reshape(rows, KVH, HEADS // KVH, HD).astype(jnp.float32)
    new_keys = new_entries[:, :KVH * HD].reshape(rows, KVH, HD).astype(jnp.float32)
    new_values = new_entries[:, KVH * HD:].reshape(rows, KVH, HD).astype(jnp.float32)
    scale = HD ** (-0.5)
    scores = jnp.einsum('rkgd,rktd->rkgt', grouped, keys.astype(jnp.float32)) * scale
    own_score = jnp.einsum('rkgd,rkd->rkg', grouped, new_keys) * scale
    position = jnp.arange(keys.shape[2], dtype=jnp.int32)
    visible = (position[None, :] < context_len[:, None])[:, None, None, :]
    scores = jnp.where(visible, scores, masked_value)
    highest = jnp.maximum(lax.optimization_barrier(jnp.max(scores, axis=-1)), own_score)
    raw_weights = jnp.where(visible, jnp.exp(scores - highest[..., None]), 0.0)
    own_raw = jnp.exp(own_score - highest)
    total = lax.optimization_barrier(jnp.sum(raw_weights, axis=-1)) + own_raw
    attention_weights = (raw_weights / total[..., None]).astype(jnp.bfloat16)
    own_weight = (own_raw / total).astype(jnp.bfloat16)
    mixed = jnp.einsum('rkgt,rktd->rkgd', attention_weights.astype(jnp.float32), values.astype(jnp.float32))
    mixed = mixed + own_weight.astype(jnp.float32)[..., None] * new_values[:, :, None, :]
    return mixed.astype(jnp.bfloat16).reshape(rows, HEADS * HD)

def layer(inputs, gain, query_weight, entry_weight, output_weight, cache, context_len):
    normed = normalize(inputs, gain)
    queries = jnp.dot(normed, query_weight, preferred_element_type=jnp.float32).astype(jnp.bfloat16)
    new_entries = jnp.dot(normed, entry_weight, preferred_element_type=jnp.float32).astype(jnp.bfloat16)
    mixed = attend(queries, new_entries, cache[:, 0], cache[:, 1], context_len)
    branch = jnp.dot(mixed, output_weight, preferred_element_type=jnp.float32)
    return (inputs.astype(jnp.float32) + branch).astype(jnp.bfloat16)

def reference(hidden_state, norm_gain, w_query, w_key_value, w_output, kv_cache, context_len):
    first = layer(hidden_state, norm_gain[0], w_query[0], w_key_value[0], w_output[0], kv_cache[0], context_len)
    second = layer(first, norm_gain[1], w_query[1], w_key_value[1], w_output[1], kv_cache[1], context_len)
    return jnp.stack([first, second])
```

```python
import jax
import jax.numpy as jnp
from jax import lax
from jax.experimental import pallas as pl
from jax.experimental.pallas import tpu as pltpu
from jax.sharding import PartitionSpec as P

MESH = pl.DeviceIdType.MESH
D = 16384
KVH = 4
HD = 128
ROWS = 128
N = 32
SHARD = 512
HALF = 256
CTX = 2048
MINE = 4
EPS = 1e-05
MASKED = -1e30
F32 = jnp.float32
BF16 = jnp.bfloat16


def arrived(ref, sem):
    pltpu.make_async_copy(ref, ref, sem).wait()


def kernel(
    hid, gain, wq_hbm, wkv_hbm, wo_hbm, kv_hbm, ctx, out,
    xg, wq, wkv, wo, kvc, qacc,
    st_send, st_recv, nk_tmp, nk_send, nk_recv, nk, q_send, q_recv, m_send, m_recv, mixed,
    s1a, r1a, s1b, r1b, s2a, r2a, s2b, r2b, s3, r3,
    load_sem, ag_send, ag_recv, rs_send, rs_recv, a2a_send, a2a_recv, relay_send, relay_recv,
):
    me = lax.axis_index("tensor")
    seg = lax.axis_index("segment")
    y, x, z = me // 8, (me // 4) % 2, me % 4

    def tid(yy, xx, zz):
        return yy * 8 + xx * 4 + zz

    def sid(h, aa, bb, xx):
        aa, bb = aa % 4, bb % 4
        return tid(bb, xx, aa) if h == 0 else tid(aa, xx, bb)

    ring = [(z, y), (y, z)]
    partner = tid(y, 1 - x, z)
    xs = jnp.where(seg == 0, x, 1 - x)

    def send(src, dst, send_sem, recv_sem, to):
        pltpu.make_async_remote_copy(
            src_ref=src, dst_ref=dst, send_sem=send_sem, recv_sem=recv_sem,
            device_id={"tensor": to}, device_id_type=MESH,
        ).start()

    loads = [
        pltpu.make_async_copy(wkv_hbm.at[0], wkv, load_sem.at[0]),
        pltpu.make_async_copy(wq_hbm.at[0], wq, load_sem.at[1]),
        pltpu.make_async_copy(kv_hbm.at[0], kvc, load_sem.at[2]),
        pltpu.make_async_copy(wo_hbm.at[0], wo, load_sem.at[3]),
    ]
    for copy in loads:
        copy.start()

    @pl.when(seg == 0)
    def _():
        for h in range(2):
            xg[h, me] = hid[:, h * HALF:(h + 1) * HALF]

    barrier = pltpu.get_barrier_semaphore()

    def greet(d, carry):
        pl.semaphore_signal(barrier, inc=1, device_id={"tensor": (me + d) % N}, device_id_type=MESH)
        return carry

    lax.fori_loop(1, N, greet, 0)
    pl.semaphore_signal(
        barrier, inc=1, device_id={"segment": 1 - seg, "tensor": partner}, device_id_type=MESH
    )
    pl.semaphore_wait(barrier, N)

    def along_b(h, j, s):
        a, b = ring[h]
        for dr in range(2):
            k = 1 + 2 * dr + j
            send(xg.at[h, s], xg.at[h, s], ag_send.at[h], ag_recv.at[h, k],
                 sid(h, a, b + 1 - 2 * dr, x))

    def along_a(h, i, s):
        a, b = ring[h]
        for dr in range(2):
            k = 9 + 8 * dr + i
            send(xg.at[h, s], xg.at[h, s], ag_send.at[h], ag_recv.at[h, k],
                 sid(h, a + 1 - 2 * dr, b, x))

    def part(h, s, dr):
        return xg.at[h, s, pl.ds(64 * dr, 64)]

    def turn(g):
        return (3 * g + 3 * ((g * (g - 1)) // 2)) % 4

    def xj(j):
        return (xs + j) % 2

    for h in range(2):
        a, b = ring[h]
        s = sid(h, a, b, xs)

        @pl.when(seg == 1)
        def _():
            arrived(xg.at[h, s], relay_recv.at[h])

        send(xg.at[h, s], xg.at[h, s], ag_send.at[h], ag_recv.at[h, 0], partner)
        along_b(h, 0, s)
        along_a(h, 0, s)

    own = tid(y, xs, z)
    total = jnp.zeros((ROWS, 1), F32)
    for h in range(2):
        v = xg[h, own].astype(F32)
        total = total + jnp.sum(v * v, axis=1, keepdims=True)
    st_send[...] = jnp.broadcast_to(total, (ROWS, 128)).T[0:8]

    def tell_stats(d, carry):
        send(st_send, st_recv.at[me], a2a_send.at[0], a2a_recv.at[0], (me + d) % N)
        return carry

    lax.fori_loop(1, N, tell_stats, 0)
    st_recv[me] = st_send[...]

    for h in range(2):
        a, b = ring[h]
        s = sid(h, a, b, 1 - xs)
        arrived(xg.at[h, s], ag_recv.at[h, 0])
        along_b(h, 1, s)
        along_a(h, 1, s)

    for j in range(2):
        for h in range(2):
            a, b = ring[h]
            for dr in range(2):
                s = sid(h, a, b - 1 + 2 * dr, xj(j))
                arrived(xg.at[h, s], ag_recv.at[h, 1 + 2 * dr + j])
                send(part(h, s, dr), part(h, s, dr), ag_send.at[h], ag_recv.at[h, 5 + 2 * dr + j],
                     sid(h, a, b + 1 - 2 * dr, x))
                along_a(h, 2 + 2 * dr + j, s)

    arrived(st_recv.at[pl.ds(0, N - 1)], a2a_recv.at[0])
    squares = jnp.sum(st_recv[...], axis=0)
    inv = lax.rsqrt(squares[0:1] * (1.0 / D) + EPS)
    inv = jnp.broadcast_to(inv, (ROWS, 128)).T
    inv = jnp.concatenate([inv, inv], axis=1)

    def normed(h, s):
        g = gain[:, pl.ds(pl.multiple_of(s * SHARD + h * HALF, HALF), HALF)].astype(F32)
        return (xg[h, s].astype(F32) * inv * g).astype(BF16)

    loads[0].wait()
    fresh = jnp.concatenate([normed(0, me), normed(1, me)], axis=1)
    for c in range(8):
        piece = jnp.dot(fresh, wkv[:, c * 128:(c + 1) * 128], preferred_element_type=F32)
        nk_tmp[pl.ds(c, ROWS, stride=8), :] = piece
    nk_send[...] = nk_tmp[...].astype(BF16).reshape(N, 32, 128)

    def tell_new(d, carry):
        to = (me + d) % N
        send(nk_send.at[to], nk_recv.at[me], a2a_send.at[1], a2a_recv.at[1], to)
        return carry

    lax.fori_loop(1, N, tell_new, 0)
    nk_recv[me] = nk_send[me]

    for j in range(2):
        for h in range(2):
            a, b = ring[h]
            s = sid(h, a, b + 2, xj(j))
            for dr in range(2):
                arrived(part(h, s, dr), ag_recv.at[h, 5 + 2 * dr + j])
            along_a(h, 6 + j, s)

    loads[1].wait()
    qacc[...] = jnp.zeros_like(qacc)

    def project(h, s):
        w = wq[pl.ds(pl.multiple_of(s * SHARD + h * HALF, HALF), HALF), :]
        return jnp.dot(normed(h, s), w, preferred_element_type=F32)

    def near(i, carry):
        for h in range(2):
            a, b = ring[h]
            bb, xx = b + turn(i // 2), xj(i % 2)
            for dr in range(2):
                s = sid(h, a - 1 + 2 * dr, bb, xx)
                arrived(xg.at[h, s], ag_recv.at[h, 9 + 8 * dr + i])
                send(part(h, s, dr), part(h, s, dr), ag_send.at[h], ag_recv.at[h, 25 + 8 * dr + i],
                     sid(h, a + 1 - 2 * dr, b, x))
            for step in (0, 3, 1):
                qacc[...] += project(h, sid(h, a + step, bb, xx))
        return carry

    lax.fori_loop(0, 8, near, 0)

    def far(i, carry):
        for h in range(2):
            a, b = ring[h]
            s = sid(h, a + 2, b + turn(i // 2), xj(i % 2))
            for dr in range(2):
                arrived(part(h, s, dr), ag_recv.at[h, 25 + 8 * dr + i])
            qacc[...] += project(h, s)
        return carry

    lax.fori_loop(0, 8, far, 0)

    queries = qacc[...].astype(BF16).astype(F32)
    for h in range(2):
        q_send[pl.ds(h, ROWS, stride=2), :] = queries[:, h * HD:(h + 1) * HD]

    def block(ref, t):
        return ref.at[pl.ds(pl.multiple_of(t * 8, 8), 8)]

    def tell_queries(d, carry):
        to = (me + d) % N
        send(block(q_send, to), block(q_recv, me), a2a_send.at[2], a2a_recv.at[2], to)
        return carry

    lax.fori_loop(1, N, tell_queries, 0)
    mine = pl.ds(pl.multiple_of(me * 8, 8), 8)
    q_recv[mine, :] = q_send[mine, :]

    arrived(nk_recv.at[pl.ds(0, N - 1)], a2a_recv.at[1])
    nk[...] = jnp.sum(nk_recv[...].astype(F32), axis=0).astype(BF16).astype(F32)

    loads[2].wait()
    arrived(q_recv.at[pl.ds(0, 8 * (N - 1))], a2a_recv.at[2])

    scale = HD ** (-0.5)

    def attend(r, carry):
        length = ctx[me * MINE + r]
        visible = lax.broadcasted_iota(jnp.int32, (16, CTX), 1) < length
        for k in range(KVH):
            q = jnp.concatenate(
                [q_recv[pl.ds(64 * k + 2 * r + h, 8, stride=8), :] for h in range(2)], axis=0
            )
            new_key = nk[pl.ds(r * 8 + k, 1), :]
            new_value = nk[pl.ds(r * 8 + 4 + k, 1), :]
            scores = lax.dot_general(
                q.astype(BF16), kvc[r, 0, k], (((1,), (1,)), ((), ())), preferred_element_type=F32
            ) * scale
            own_score = jnp.sum(q * new_key, axis=1, keepdims=True) * scale
            scores = jnp.where(visible, scores, MASKED)
            highest = jnp.maximum(jnp.max(scores, axis=1, keepdims=True), own_score)
            raw = jnp.where(visible, jnp.exp(scores - highest), 0.0)
            own_raw = jnp.exp(own_score - highest)
            denom = jnp.sum(raw, axis=1, keepdims=True) + own_raw
            weights = (raw / denom).astype(BF16)
            own_weight = (own_raw / denom).astype(BF16).astype(F32)
            mix = jnp.dot(weights, kvc[r, 1, k], preferred_element_type=F32)
            mix = (mix + own_weight * new_value).astype(BF16).astype(F32)
            for h in range(2):
                m_send[pl.ds(64 * k + 2 * r + h, 8, stride=8), :] = mix[8 * h:8 * h + 8]
        return carry

    lax.fori_loop(0, MINE, attend, 0)

    def tell_mixed(d, carry):
        to = (me + d) % N
        send(block(m_send, to), block(m_recv, me), a2a_send.at[3], a2a_recv.at[3], to)
        return carry

    lax.fori_loop(1, N, tell_mixed, 0)
    m_recv[mine, :] = m_send[mine, :]
    loads[3].wait()
    arrived(m_recv.at[pl.ds(0, 8 * (N - 1))], a2a_recv.at[3])
    for h in range(2):
        mixed[:, h * HD:(h + 1) * HD] = m_recv[pl.ds(h, ROWS, stride=2), :].astype(BF16)

    def partial(h, s):
        w = wo[:, pl.ds(pl.multiple_of(s * SHARD + h * HALF, HALF), HALF)]
        return jnp.dot(mixed[...], w, preferred_element_type=F32)

    def place(b, i):
        return b + turn(3 - i // 2), (x + 1 + i % 2) % 2

    def opposite(i, carry):
        for h in range(2):
            a, b = ring[h]
            bb, xx = place(b, i)
            s1a[h, i] = partial(h, sid(h, a + 2, bb, xx)).astype(BF16)
            for dr in range(2):
                send(s1a.at[h, i, pl.ds(64 * dr, 64)], r1a.at[h, dr, i], rs_send.at[h],
                     rs_recv.at[h, 8 * dr + i], sid(h, a + 1 - 2 * dr, b, x))
        return carry

    lax.fori_loop(0, 8, opposite, 0)

    def merged(value, extra, dr):
        top, low = value[0:64], value[64:128]
        if dr == 0:
            top = top + extra.astype(F32)
        else:
            low = low + extra.astype(F32)
        return jnp.concatenate([top, low], axis=0)

    def beside(i, carry):
        for h in range(2):
            a, b = ring[h]
            bb, xx = place(b, i)
            for dr in range(2):
                value = partial(h, sid(h, a + 1 - 2 * dr, bb, xx))
                arrived(r1a.at[h, dr, i], rs_recv.at[h, 8 * dr + i])
                s1b[h, dr, i] = merged(value, r1a[h, dr, i], dr).astype(BF16)
                send(s1b.at[h, dr, i], r1b.at[h, dr, i], rs_send.at[h],
                     rs_recv.at[h, 16 + 8 * dr + i], sid(h, a + 1 - 2 * dr, b, x))
        return carry

    lax.fori_loop(0, 8, beside, 0)

    def first_ring(h, i):
        a, b = ring[h]
        bb, xx = place(b, i)
        value = partial(h, sid(h, a, bb, xx))
        for dr in range(2):
            arrived(r1b.at[h, dr, i], rs_recv.at[h, 16 + 8 * dr + i])
            value = value + r1b[h, dr, i].astype(F32)
        return value

    def second_opposite(j, carry):
        for h in range(2):
            a, b = ring[h]
            s2a[h, j] = first_ring(h, j).astype(BF16)
            for dr in range(2):
                send(s2a.at[h, j, pl.ds(64 * dr, 64)], r2a.at[h, dr, j], rs_send.at[h],
                     rs_recv.at[h, 32 + 2 * dr + j], sid(h, a, b + 1 - 2 * dr, x))
        return carry

    lax.fori_loop(0, 2, second_opposite, 0)

    def second_beside(j, carry):
        for dr in range(2):
            for h in range(2):
                a, b = ring[h]
                value = first_ring(h, 2 + 2 * dr + j)
                arrived(r2a.at[h, dr, j], rs_recv.at[h, 32 + 2 * dr + j])
                s2b[h, dr, j] = merged(value, r2a[h, dr, j], dr).astype(BF16)
                send(s2b.at[h, dr, j], r2b.at[h, dr, j], rs_send.at[h],
                     rs_recv.at[h, 36 + 2 * dr + j], sid(h, a, b + 1 - 2 * dr, x))
        return carry

    lax.fori_loop(0, 2, second_beside, 0)

    def second_ring(h, j):
        value = first_ring(h, 6 + j)
        for dr in range(2):
            arrived(r2b.at[h, dr, j], rs_recv.at[h, 36 + 2 * dr + j])
            value = value + r2b[h, dr, j].astype(F32)
        return value

    for h in range(2):
        s3[h] = second_ring(h, 0).astype(BF16)
        send(s3.at[h], r3.at[h], rs_send.at[h], rs_recv.at[h, 40], partner)
    for h in range(2):
        value = second_ring(h, 1)
        arrived(r3.at[h], rs_recv.at[h, 40])
        value = value + r3[h].astype(F32) + xg[h, me].astype(F32)
        out[0, :, h * HALF:(h + 1) * HALF] = value.astype(BF16)
        s3[h + 2] = value.astype(BF16)

        @pl.when(seg == 0)
        def _():
            pltpu.make_async_remote_copy(
                src_ref=s3.at[h + 2], dst_ref=xg.at[h, me],
                send_sem=relay_send.at[h], recv_sem=relay_recv.at[h],
                device_id={"segment": 1, "tensor": partner}, device_id_type=MESH,
            ).start()

    for h in range(2):
        blocks = xg.at[h, pl.ds(0, N - 1)]
        arrived(blocks, ag_send.at[h])
        arrived(blocks, rs_send.at[h])

        @pl.when(seg == 0)
        def _():
            arrived(s3.at[h + 2], relay_send.at[h])

    arrived(st_recv.at[pl.ds(0, N - 1)], a2a_send.at[0])
    arrived(nk_recv.at[pl.ds(0, N - 1)], a2a_send.at[1])
    arrived(q_recv.at[pl.ds(0, 8 * (N - 1))], a2a_send.at[2])
    arrived(m_recv.at[pl.ds(0, 8 * (N - 1))], a2a_send.at[3])


def body(hidden_state, norm_gain, w_query, w_key_value, w_output, kv_cache, context_len):
    vmem = pl.BlockSpec(memory_space=pltpu.VMEM)
    hbm = pl.BlockSpec(memory_space=pl.ANY)
    dma = pltpu.SemaphoreType.DMA
    return pl.pallas_call(
        kernel,
        out_shape=jax.ShapeDtypeStruct((1, ROWS, SHARD), BF16),
        in_specs=[vmem, vmem, hbm, hbm, hbm, hbm, pl.BlockSpec(memory_space=pltpu.SMEM)],
        out_specs=vmem,
        scratch_shapes=[
            pltpu.VMEM((2, N, ROWS, HALF), BF16),
            pltpu.VMEM((D, 2 * HD), BF16),
            pltpu.VMEM((SHARD, 2 * KVH * HD), BF16),
            pltpu.VMEM((2 * HD, D), BF16),
            pltpu.VMEM((MINE, 2, KVH, CTX, HD), BF16),
            pltpu.VMEM((ROWS, 2 * HD), F32),
            pltpu.VMEM((8, 128), F32),
            pltpu.VMEM((N, 8, 128), F32),
            pltpu.VMEM((ROWS * 8, 128), F32),
            pltpu.VMEM((N, 32, 128), BF16),
            pltpu.VMEM((N, 32, 128), BF16),
            pltpu.VMEM((32, 128), F32),
            pltpu.VMEM((N * 8, 128), F32),
            pltpu.VMEM((N * 8, 128), F32),
            pltpu.VMEM((N * 8, 128), F32),
            pltpu.VMEM((N * 8, 128), F32),
            pltpu.VMEM((ROWS, 2 * HD), BF16),
            pltpu.VMEM((2, 8, ROWS, HALF), BF16),
            pltpu.VMEM((2, 2, 8, ROWS // 2, HALF), BF16),
            pltpu.VMEM((2, 2, 8, ROWS, HALF), BF16),
            pltpu.VMEM((2, 2, 8, ROWS, HALF), BF16),
            pltpu.VMEM((2, 2, ROWS, HALF), BF16),
            pltpu.VMEM((2, 2, 2, ROWS // 2, HALF), BF16),
            pltpu.VMEM((2, 2, 2, ROWS, HALF), BF16),
            pltpu.VMEM((2, 2, 2, ROWS, HALF), BF16),
            pltpu.VMEM((4, ROWS, HALF), BF16),
            pltpu.VMEM((2, ROWS, HALF), BF16),
            dma((4,)),
            dma((2,)),
            dma((2, 41)),
            dma((2,)),
            dma((2, 41)),
            dma((4,)),
            dma((4,)),
            dma((2,)),
            dma((2,)),
        ],
        compiler_params=pltpu.CompilerParams(
            collective_id=0, has_side_effects=True, vmem_limit_bytes=60 * 1024 * 1024
        ),
    )(hidden_state, norm_gain, w_query, w_key_value, w_output, kv_cache, context_len)


def solution(mesh):
    placed = (
        P("dp", "tensor"),
        P("segment", None),
        P("segment", None, "tensor"),
        P("segment", "tensor", None),
        P("segment", "tensor", None),
        P("segment", ("dp", "tensor"), None, None, None, None),
        P("dp"),
    )
    return jax.shard_map(
        body, mesh=mesh, in_specs=placed, out_specs=P("segment", "dp", "tensor"), check_vma=False
    )
```
